1024 devices in a mesh: grp: 64 (over x, z), sp: 16 (over y, core).
Axes of the slice: x: 8, y: 8, z: 8, core: 2. Of those that a mesh axis runs over, the one named last changes fastest.
Arguments:
- stay_qkv: bfloat16 [64, 2048, 3, 2048], P('grp', 'sp'), may hold values from -6 to 6
- outbox_qkv: bfloat16 [64, 128, 3, 2048], P('grp', 'sp'), may hold values from -6 to 6
- stay_clip: int32 [64, 2048], P('grp'), may hold values from 0 to 7, never falling along the last dimension, each value on 1 to 1024 neighbouring positions
- out_len: int32 [128], replicated, may hold values from 1 to 64, 6144 in all
- out_place: int32 [128], replicated, may hold values from 0 to 127, each once
Outputs:
- attn_stay: bfloat16 [64, 2048, 2048], P('grp', 'sp')
- attn_inbox: bfloat16 [64, 128, 2048], P('grp', 'sp')
The draws below stay inside these ranges and needn't reach their ends.
Inputs may be any that keep to these rules, and one draw needn't show every extreme that they name: Each value appears once: clip j of group g goes to group out_place[2 g + j] // 2, inbox half out_place[2 g + j] % 2. Clip j of group g fills outbox rows j * 64 to j * 64 + out_len[2 g + j] - 1; the other rows of the half are unused. `stay_clip`: never falls along a group's tokens.
All inputs are finite; a program needn't handle non-finite values.
Results may differ from the reference program's by a relative error of at most 0.0043.
Values may be sent and summed in bfloat16 or wider, within the bound.
No kernel may reach another device: no remote copies, remote signals or barrier semaphores. Data moves between devices by JAX's collectives and lax.ppermute only.
A program may use at most 32 MiB of HBM per device.

```python
import math
import jax
import jax.numpy as jnp
import numpy as np
from jax import lax

HEADS = 16
HD = 128
TOK_DEV = 128
GTOK = 2048
OUT = 128
HALF = 64
N_GRP = 64


def aligned_rows(key, groups, token_rows, strength):
    base_key, sign_key, level_key = jax.random.split(key, 3)
    base = jax.random.normal(base_key, (groups, token_rows, 3, HEADS * HD), jnp.float32)
    base = jnp.clip(base, -6.0, 6.0)
    pattern = jnp.where(jax.random.normal(sign_key, (groups, token_rows, HEADS * HD), jnp.float32) >= 0.0, 1.0, -1.0)
    level = jax.random.uniform(level_key, (groups, token_rows, 1), jnp.float32, 3.5, 5.0)
    aligned = level * pattern
    previous = jnp.roll(aligned, 1, axis=1) * 0.99
    position = jnp.arange(token_rows)[None, :, None]
    lead_hit = (position % 61 == 5) & (strength > 0.0)
    next_hit = (position % 61 == 6) & (strength > 0.0)
    queries = jnp.where(lead_hit, aligned, base[:, :, 0])
    key_rows = jnp.where(lead_hit, aligned, jnp.where(next_hit, previous, base[:, :, 1]))
    stacked = jnp.stack([queries, key_rows, base[:, :, 2]], axis=2)
    return stacked.astype(jnp.bfloat16)


def draw_stay_qkv(key, part):
    key = jax.random.fold_in(key, 11)
    return aligned_rows(key, N_GRP, GTOK, 0.0)


def draw_outbox_qkv(key, part):
    key = jax.random.fold_in(key, 23)
    return aligned_rows(key, N_GRP, OUT, 0.0)


def profile(number_of, total, reach, skew):
    weights = [(1 << 20) // math.isqrt(grade ** skew) + 1 for grade in range(2, number_of + 1)]
    spare, holding = total - reach - (number_of - 1), [1] * (number_of - 1)
    while spare > 0:
        movable = [i for i in range(number_of - 1) if holding[i] < reach]
        whole, left = sum([weights[i] for i in movable]), spare
        for i in movable:
            addition = min(reach - holding[i], max(1, left * weights[i] // whole), spare)
            holding[i] = holding[i] + addition
            spare = spare - addition
    return np.array([reach] + holding)


def ragged(key, number_of, total, bound, lean):
    if number_of == 2:
        one = jax.random.randint(key, (), max(1, total - bound), min(bound, total - 1) + 1)
        return jnp.stack([one, total - one])
    sizes = jnp.asarray(profile(number_of, total, bound, lean), jnp.int32)
    twos = (number_of - 1) // 2
    donor, taker = sizes[1:1 + 2 * twos:2], sizes[2:2 + 2 * twos:2]
    room = jnp.minimum(donor - 1, bound - taker)
    passed = jax.random.randint(jax.random.fold_in(key, 1), (twos,), 0, 1 << 20) % (room + 1)
    sizes = sizes.at[1:1 + 2 * twos:2].set(donor - passed).at[2:2 + 2 * twos:2].set(taker + passed)
    return sizes[jax.random.permutation(jax.random.fold_in(key, 2), number_of)]


def setup_inputs(seed: int = 0) -> dict:
    arg_keys = jax.random.split(jax.random.key(seed), 6)
    stay_qkv = draw_stay_qkv(jax.random.fold_in(arg_keys[5], 71), 0)
    outbox_qkv = draw_outbox_qkv(jax.random.fold_in(arg_keys[5], 71), 0)
    stay_clip = jax.vmap(lambda own: jnp.searchsorted(jnp.cumsum(ragged(own, 8, GTOK, GTOK // 2, 2)), jnp.arange(GTOK), side="right"))(jax.random.split(arg_keys[2], N_GRP)).reshape((N_GRP, GTOK)).astype(jnp.int32)
    out_len = ragged(arg_keys[3], 2 * N_GRP, 3 * N_GRP * TOK_DEV // 4, HALF, 1).astype(jnp.int32)
    out_place = jax.random.permutation(arg_keys[4], 2 * N_GRP).astype(jnp.int32)
    return dict(stay_qkv=stay_qkv, outbox_qkv=outbox_qkv, stay_clip=stay_clip, out_len=out_len, out_place=out_place)


def attend(queries, key_rows, values, allowed):
    factor = 1.0 / math.sqrt(HD)
    scores = jnp.einsum('qhd,khd->hqk', queries.astype(jnp.float32), key_rows.astype(jnp.float32)) * factor
    scores = jnp.where(allowed[None], scores, -1e+30)
    row_peak = lax.optimization_barrier(jnp.max(scores, axis=2, keepdims=True))
    weights = jnp.exp(scores - row_peak)
    totals = lax.optimization_barrier(jnp.sum(weights, axis=2))
    rounded = weights.astype(jnp.bfloat16)
    blended = jnp.einsum('hqk,khd->qhd', rounded.astype(jnp.float32), values.astype(jnp.float32))
    return blended / jnp.transpose(totals)[:, :, None]

def reference(stay_qkv, outbox_qkv, stay_clip, out_len, out_place):
    clip_slots = jnp.arange(2 * N_GRP, dtype=jnp.int32)

    def group_out(group_index):
        stay_rows = stay_qkv[group_index].reshape(GTOK, 3, HEADS, HD)
        segment = stay_clip[group_index]
        allowed = segment[:, None] == segment[None, :]
        stay_result = attend(stay_rows[:, 0], stay_rows[:, 1], stay_rows[:, 2], allowed)
        stay_result = stay_result.astype(jnp.bfloat16).reshape(GTOK, HEADS * HD)
        halves = []
        for half_index in range(2):
            chosen = (out_place == 2 * group_index + half_index).astype(jnp.int32)
            clip_index = jnp.sum(chosen * clip_slots).astype(jnp.int32)
            length = jnp.sum(chosen * out_len).astype(jnp.int32)
            source = (clip_index // 2).astype(jnp.int32)
            offset = (clip_index % 2 * HALF).astype(jnp.int32)
            zero_index = jnp.zeros((), jnp.int32)
            token_rows = lax.dynamic_slice(outbox_qkv, (source, offset, zero_index, zero_index), (1, HALF, 3, HEADS * HD))
            token_rows = token_rows[0].reshape(HALF, 3, HEADS, HD)
            position = jnp.arange(HALF, dtype=jnp.int32)
            usable = position < length
            allowed_half = usable[:, None] & usable[None, :]
            result = attend(token_rows[:, 0], token_rows[:, 1], token_rows[:, 2], allowed_half)
            result = jnp.where(usable[:, None, None], result, jnp.zeros_like(result)).astype(jnp.bfloat16)
            halves.append(result.reshape(HALF, HEADS * HD))
        return (stay_result, jnp.concatenate(halves, axis=0))
    attn_stay, attn_inbox = lax.map(group_out, jnp.arange(N_GRP, dtype=jnp.int32))
    return (attn_stay, attn_inbox)
```

```python
import math

import jax
import jax.numpy as jnp
from jax import lax
from jax.experimental import pallas as pl
from jax.experimental.pallas import tpu as pltpu
from jax.sharding import Mesh
from jax.sharding import PartitionSpec as P

HEADS = 16
HD = 128
HALF = 64
ROWS = 256
BLOCKS = 8
WIDTHS = (2, 4, 5, 6, 8)
SCALE = math.log2(math.e) / math.sqrt(HD)
GRP = ("x", "z")
SP = ("y", "c")


def stay_kernel(low_ref, pick_ref, rows_ref, key_clip_ref, query_clip_ref, out_ref):
    def block(index, carry):
        queries = rows_ref[pl.ds(2 * index, 2), 0].reshape(ROWS, HD)
        query_clip = query_clip_ref[pl.ds(pl.multiple_of(index * ROWS, ROWS), ROWS), :]
        low = low_ref[index]

        def width(count):
            def run():
                scores, peak = [], None
                for j in range(count):
                    keys = rows_ref[pl.ds(2 * (low + j), 2), 1].reshape(ROWS, HD)
                    product = lax.dot_general(
                        queries, keys, (((1,), (1,)), ((), ())), preferred_element_type=jnp.float32
                    )
                    key_clip = key_clip_ref[low + j]
                    for part in (slice(0, HD), slice(HD, 2 * HD)):
                        score = jnp.where(query_clip == key_clip[:, part], product[:, part], -1e30)
                        peak = score if peak is None else jnp.maximum(peak, score)
                        scores.append(score)
                peak = jnp.broadcast_to(jnp.max(peak, axis=1, keepdims=True), (ROWS, HD))
                totals, blended = 0.0, 0.0
                for j in range(count):
                    left = jnp.exp2((scores[2 * j] - peak) * SCALE)
                    right = jnp.exp2((scores[2 * j + 1] - peak) * SCALE)
                    totals = totals + (left + right)
                    rounded = jnp.concatenate([left, right], axis=1).astype(jnp.bfloat16)
                    values = rows_ref[pl.ds(2 * (low + j), 2), 2].reshape(ROWS, HD)
                    blended = blended + jnp.dot(
                        rounded, values, preferred_element_type=jnp.float32
                    )
                result = blended / jnp.sum(totals, axis=1, keepdims=True)
                out_ref[pl.ds(2 * index, 2), 0:HD, :] = result.astype(jnp.bfloat16).reshape(
                    2, HD, HD
                )

            return run

        for number, count in enumerate(WIDTHS):
            pl.when(pick_ref[index] == number)(width(count))
        return carry

    lax.fori_loop(0, BLOCKS, block, 0)


def stay_plan(clip):
    blocks = clip.reshape(BLOCKS, ROWS)
    first, last = blocks[:, :1], blocks[:, -1:]
    low = jnp.sum((clip[None, :] < first).astype(jnp.int32), axis=1) // ROWS
    high = (jnp.sum((clip[None, :] <= last).astype(jnp.int32), axis=1) + ROWS - 1) // ROWS
    need = high - low
    pick = sum((need > count).astype(jnp.int32) for count in WIDTHS)
    count = sum(jnp.where(pick == number, value, 0) for number, value in enumerate(WIDTHS))
    key_clip = clip.reshape(BLOCKS, 1, ROWS)
    query_clip = jnp.broadcast_to(clip[:, None], (clip.shape[0], HD))
    return jnp.minimum(low, BLOCKS - count), pick, key_clip, query_clip


def stay_attention(plan, rows):
    smem, vmem = pl.BlockSpec(memory_space=pltpu.SMEM), pl.BlockSpec(memory_space=pltpu.VMEM)
    return pl.pallas_call(
        stay_kernel,
        out_shape=jax.ShapeDtypeStruct((HEADS, HD + 8, HD), jnp.bfloat16),
        in_specs=[smem, smem, vmem, vmem, vmem],
        out_specs=vmem,
        compiler_params=pltpu.CompilerParams(vmem_limit_bytes=40 * 2**20),
        name="stay_attention",
    )(plan[0], plan[1], rows, plan[2], plan[3])


def box_attention(rows, lengths):
    row = jnp.arange(2 * HALF, dtype=jnp.int32)
    usable = row % HALF < jnp.where(row < HALF, lengths[0], lengths[1])
    half = row // HALF
    allowed = (half[:, None] == half[None, :]) & usable[:, None] & usable[None, :]
    scores = lax.dot_general(
        rows[0], rows[1], (((1,), (1,)), ((), ())), preferred_element_type=jnp.float32
    )
    scores = jnp.where(allowed, scores, -1e30)
    weights = jnp.exp2((scores - jnp.max(scores, axis=1, keepdims=True)) * SCALE)
    totals = jnp.sum(weights, axis=1, keepdims=True)
    blended = jnp.dot(weights.astype(jnp.bfloat16), rows[2], preferred_element_type=jnp.float32)
    return jnp.where(usable[:, None], blended / totals, 0.0).astype(jnp.bfloat16)


def select_kernel(place_ref, here_ref, gathered_ref, slots_ref):
    x, z, c = here_ref[0], here_ref[1], here_ref[2]
    slots_ref[...] = jnp.zeros_like(slots_ref)
    for source in range(16):
        place = place_ref[2 * ((source // 2) * 8 + z) + source % 2]
        far = (place // 2) % 8 ^ z
        slot = (far % 2) * 8 + (far // 2 % 2) * 4 + (far // 4) * 2 + place % 2

        @pl.when(place // 16 == x)
        def _(source=source, slot=slot):
            clip = gathered_ref[2 * (source // 2) + c, source % 2]
            slots_ref[slot] = clip


def select(place, here, gathered):
    smem, vmem = pl.BlockSpec(memory_space=pltpu.SMEM), pl.BlockSpec(memory_space=pltpu.VMEM)
    return pl.pallas_call(
        select_kernel,
        out_shape=jax.ShapeDtypeStruct((16, HALF, HD), jnp.bfloat16),
        in_specs=[smem, smem, vmem],
        out_specs=vmem,
        name="select_clips",
    )(place, here, gathered)


def local(stay_qkv, outbox_qkv, stay_clip, out_len, out_place):
    x, z, c = lax.axis_index("x"), lax.axis_index("z"), lax.axis_index("c")
    group = x * 8 + z
    clip = stay_clip[0]

    box = jnp.transpose(outbox_qkv[0].reshape(8, 3, HEADS, HD), (2, 1, 0, 3))
    box = lax.all_to_all(box.reshape(HEADS, 24, HD), SP, split_axis=0, concat_axis=0, tiled=True)
    stay = jnp.transpose(stay_qkv[0].reshape(HD, 3, HEADS, HD), (2, 1, 0, 3))
    box, stay = lax.optimization_barrier((box, stay))
    stay = lax.all_to_all(
        stay.reshape(HEADS, 3 * HD, HD), SP, split_axis=0, concat_axis=0, tiled=True
    )

    box = jnp.transpose(box.reshape(HEADS, 3, 8, HD), (1, 0, 2, 3)).reshape(3, 2 * HALF, HD)
    lengths = lax.dynamic_slice_in_dim(out_len, 2 * group, 2)
    box_out = box_attention(box, lengths)

    gathered = lax.all_gather(box_out, ("x", "c"), axis=0, tiled=True)
    slots = select(out_place, jnp.stack([x, z, c]), gathered.reshape(16, 2, HALF, HD))
    for bit in (1, 2, 4):
        half = slots.shape[0] // 2
        came = lax.ppermute(slots[half:], "z", [(i, i ^ bit) for i in range(8)])
        slots = slots[:half] + came
    inbox = slots.reshape(HEADS, 8, HD)

    out = stay_attention(stay_plan(clip), stay.reshape(HEADS, 3, HD, HD))
    out = lax.dynamic_update_slice(out, inbox, (0, HD, 0))
    back = lax.all_to_all(out, SP, split_axis=0, concat_axis=0, tiled=True)
    stay_back = jnp.transpose(back[:, :HD], (1, 0, 2)).reshape(1, HD, HEADS * HD)
    inbox_back = jnp.transpose(back[:, HD:], (1, 0, 2)).reshape(1, 8, HEADS * HD)
    return stay_back, inbox_back


def solution(mesh):
    lines = Mesh(mesh.devices.reshape(8, 8, 8, 2), ("x", "z", "y", "c"))
    in_specs = (P(GRP, SP, None, None), P(GRP, SP, None, None), P(GRP, None), P(), P())
    out_specs = (P(GRP, SP, None), P(GRP, SP, None))
    return jax.shard_map(local, mesh=lines, in_specs=in_specs, out_specs=out_specs, check_vma=False)
```

```python
import math

import jax
import jax.numpy as jnp
from jax import lax
from jax.experimental import pallas as pl
from jax.experimental.layout import Layout, with_layout_constraint
from jax.experimental.pallas import tpu as pltpu
from jax.sharding import Mesh
from jax.sharding import PartitionSpec as P

HEADS = 16
HD = 128
HALF = 64
ROWS = 256
BLOCKS = 8
WIDTHS = (2, 4, 5, 6, 8)
SCALE = math.log2(math.e) / math.sqrt(HD)
GRP = ("x", "z")
SP = ("y", "c")


def stay_kernel(low_ref, pick_ref, rows_ref, key_clip_ref, query_clip_ref, out_ref):
    def block(index, carry):
        queries = rows_ref[pl.ds(2 * index, 2), 0].reshape(ROWS, HD)
        query_clip = query_clip_ref[pl.ds(pl.multiple_of(index * ROWS, ROWS), ROWS), :]
        low = low_ref[index]

        def width(count):
            def run():
                scores, peak = [], None
                for j in range(count):
                    keys = rows_ref[pl.ds(2 * (low + j), 2), 1].reshape(ROWS, HD)
                    product = lax.dot_general(
                        queries, keys, (((1,), (1,)), ((), ())), preferred_element_type=jnp.float32
                    )
                    key_clip = key_clip_ref[low + j]
                    for part in (slice(0, HD), slice(HD, 2 * HD)):
                        score = jnp.where(query_clip == key_clip[:, part], product[:, part], -1e30)
                        peak = score if peak is None else jnp.maximum(peak, score)
                        scores.append(score)
                peak = jnp.broadcast_to(jnp.max(peak, axis=1, keepdims=True), (ROWS, HD))
                totals, blended = 0.0, 0.0
                for j in range(count):
                    left = jnp.exp2((scores[2 * j] - peak) * SCALE)
                    right = jnp.exp2((scores[2 * j + 1] - peak) * SCALE)
                    totals = totals + (left + right)
                    rounded = jnp.concatenate([left, right], axis=1).astype(jnp.bfloat16)
                    values = rows_ref[pl.ds(2 * (low + j), 2), 2].reshape(ROWS, HD)
                    blended = blended + jnp.dot(
                        rounded, values, preferred_element_type=jnp.float32
                    )
                result = blended / jnp.sum(totals, axis=1, keepdims=True)
                out_ref[pl.ds(2 * index, 2), 0:HD, :] = result.astype(jnp.bfloat16).reshape(
                    2, HD, HD
                )

            return run

        for number, count in enumerate(WIDTHS):
            pl.when(pick_ref[index] == number)(width(count))
        return carry

    lax.fori_loop(0, BLOCKS, block, 0)


def stay_plan(clip):
    blocks = clip.reshape(BLOCKS, ROWS)
    first, last = blocks[:, :1], blocks[:, -1:]
    low = jnp.sum((clip[None, :] < first).astype(jnp.int32), axis=1) // ROWS
    high = (jnp.sum((clip[None, :] <= last).astype(jnp.int32), axis=1) + ROWS - 1) // ROWS
    need = high - low
    pick = sum((need > count).astype(jnp.int32) for count in WIDTHS)
    count = sum(jnp.where(pick == number, value, 0) for number, value in enumerate(WIDTHS))
    key_clip = clip.reshape(BLOCKS, 1, ROWS)
    query_clip = jnp.broadcast_to(clip[:, None], (clip.shape[0], HD))
    return jnp.minimum(low, BLOCKS - count), pick, key_clip, query_clip


def stay_attention(plan, rows):
    smem, vmem = pl.BlockSpec(memory_space=pltpu.SMEM), pl.BlockSpec(memory_space=pltpu.VMEM)
    return pl.pallas_call(
        stay_kernel,
        out_shape=jax.ShapeDtypeStruct((HEADS, HD + 8, HD), jnp.bfloat16),
        in_specs=[smem, smem, vmem, vmem, vmem],
        out_specs=vmem,
        compiler_params=pltpu.CompilerParams(vmem_limit_bytes=40 * 2**20),
        name="stay_attention",
    )(plan[0], plan[1], rows, plan[2], plan[3])


def split_kernel(rows_ref, heads_ref):
    for head in range(HEADS):
        heads_ref[head, 0] = rows_ref[0, :, head * HD : (head + 1) * HD]


def split_heads(rows):
    tokens = rows.shape[1]
    return pl.pallas_call(
        split_kernel,
        grid=(3,),
        out_shape=jax.ShapeDtypeStruct((HEADS, 3, tokens, HD), rows.dtype),
        in_specs=[pl.BlockSpec((1, tokens, HEADS * HD), lambda t: (t, 0, 0))],
        out_specs=pl.BlockSpec((HEADS, 1, tokens, HD), lambda t: (0, t, 0, 0)),
        compiler_params=pltpu.CompilerParams(vmem_limit_bytes=8 * 2**20),
        name="split_heads",
    )(rows)


def box_mask(out_len):
    group = lax.axis_index("x") * 8 + lax.axis_index("z")
    lengths = lax.dynamic_slice_in_dim(out_len, 2 * group, 2)
    row = jnp.arange(2 * HALF, dtype=jnp.int32)
    usable = row % HALF < jnp.where(row < HALF, lengths[0], lengths[1])
    half = row // HALF
    allowed = (half[:, None] == half[None, :]) & usable[:, None] & usable[None, :]
    return jnp.broadcast_to(usable[:, None], allowed.shape).astype(jnp.float32), jnp.where(
        allowed, 0.0, 1.0
    )


def box_attention(masks, rows):
    usable, blocked = masks
    queries, keys, values = (rows[:, t].reshape(2 * HALF, HD) for t in range(3))
    scores = lax.dot_general(
        queries, keys, (((1,), (1,)), ((), ())), preferred_element_type=jnp.float32
    )
    scores = jnp.where(blocked > 0.0, -1e30, scores)
    weights = jnp.exp2((scores - jnp.max(scores, axis=1, keepdims=True)) * SCALE)
    totals = jnp.sum(weights, axis=1, keepdims=True)
    blended = jnp.dot(weights.astype(jnp.bfloat16), values, preferred_element_type=jnp.float32)
    result = jnp.where(usable > 0.0, blended / totals, 0.0).astype(jnp.bfloat16)
    return with_layout_constraint(result, Layout(major_to_minor=(0, 1)))


def select_kernel(place_ref, gathered_ref, keep_ref, send_ref):
    x, z, c = lax.axis_index("x"), lax.axis_index("z"), lax.axis_index("c")
    keep_ref[...] = jnp.zeros_like(keep_ref)
    send_ref[...] = jnp.zeros_like(send_ref)
    for source in range(16):
        place = place_ref[2 * ((source // 2) * 8 + z) + source % 2]
        far = (place // 2) % 8 ^ z
        slot = (far // 2 % 2) * 4 + (far // 4) * 2 + place % 2
        mine = place // 16 == x
        for odd, slots_ref in enumerate((keep_ref, send_ref)):

            @pl.when(mine & (far % 2 == odd))
            def _(source=source, slot=slot, slots_ref=slots_ref):
                slots_ref[slot] = gathered_ref[2 * (source // 2) + c, source % 2]


def select(place, gathered):
    smem, vmem = pl.BlockSpec(memory_space=pltpu.SMEM), pl.BlockSpec(memory_space=pltpu.VMEM)
    return pl.pallas_call(
        select_kernel,
        out_shape=[jax.ShapeDtypeStruct((8, HALF, HD), jnp.bfloat16)] * 2,
        in_specs=[smem, vmem],
        out_specs=[vmem] * 2,
        compiler_params=pltpu.CompilerParams(vmem_limit_bytes=4 * 2**20),
        name="select_clips",
    )(place, gathered)


def swap(rows, bit):
    return lax.ppermute(rows, "z", [(i, i ^ bit) for i in range(8)])


def local(stay_qkv, outbox_qkv, stay_clip, out_len, out_place):
    masks = box_mask(out_len)
    box = jnp.transpose(outbox_qkv[0].reshape(8, 3, HEADS, HD), (2, 1, 0, 3))
    box = lax.all_to_all(box.reshape(HEADS, 24, HD), SP, split_axis=0, concat_axis=0, tiled=True)
    stay = split_heads(jnp.transpose(stay_qkv[0], (1, 0, 2)))
    box, stay, masks = lax.optimization_barrier((box, stay, masks))
    stay = lax.all_to_all(
        stay.reshape(HEADS, 3 * HD, HD), SP, split_axis=0, concat_axis=0, tiled=True
    )

    box_out = box_attention(masks, box.reshape(HEADS, 3, 8, HD))

    gathered = lax.all_gather(box_out, ("x", "c"), axis=0, tiled=True)
    keep, send = select(out_place, gathered.reshape(16, 2, HALF, HD))
    slots = keep + swap(send, 1)
    slots, clip = lax.optimization_barrier((slots, stay_clip[0]))
    plan = stay_plan(clip)
    slots = slots[:4] + swap(slots[4:], 2)
    slots, stay, plan = lax.optimization_barrier((slots, stay, plan))
    slots = slots[:2] + swap(slots[2:], 4)
    out = stay_attention(plan, stay.reshape(HEADS, 3, HD, HD))

    out = lax.dynamic_update_slice(out, slots.reshape(HEADS, 8, HD), (0, HD, 0))
    back = lax.all_to_all(out, SP, split_axis=0, concat_axis=0, tiled=True)
    stay_back = jnp.transpose(back[:, :HD], (1, 0, 2)).reshape(1, HD, HEADS * HD)
    inbox_back = jnp.transpose(back[:, HD:], (1, 0, 2)).reshape(1, 8, HEADS * HD)
    return stay_back, inbox_back


def solution(mesh):
    lines = Mesh(mesh.devices.reshape(8, 8, 8, 2), ("x", "z", "y", "c"))
    in_specs = (P(GRP, SP, None, None), P(GRP, SP, None, None), P(GRP, None), P(), P())
    out_specs = (P(GRP, SP, None), P(GRP, SP, None))
    return jax.shard_map(local, mesh=lines, in_specs=in_specs, out_specs=out_specs, check_vma=False)
```

```python
import math

import jax
import jax.numpy as jnp
from jax import lax
from jax.experimental import pallas as pl
from jax.experimental.layout import Layout, with_layout_constraint
from jax.experimental.pallas import tpu as pltpu
from jax.sharding import Mesh
from jax.sharding import PartitionSpec as P

HEADS = 16
HD = 128
HALF = 64
ROWS = 256
BLOCKS = 8
WIDTHS = (2, 3, 4, 5, 6, 8)
SCALE = math.log2(math.e) / math.sqrt(HD)
GRP = ("x", "z")
SP = ("y", "c")


def stay_kernel(low_ref, pick_ref, rows_ref, key_clip_ref, query_clip_ref, out_ref):
    def score(index, count):
        queries = rows_ref[pl.ds(2 * index, 2), 0].reshape(ROWS, HD)
        query_clip = query_clip_ref[pl.ds(pl.multiple_of(index * ROWS, ROWS), ROWS), :]
        low = low_ref[index]
        scores, peak = [], None
        for j in range(count):
            keys = rows_ref[pl.ds(2 * (low + j), 2), 1].reshape(ROWS, HD)
            product = lax.dot_general(
                queries, keys, (((1,), (1,)), ((), ())), preferred_element_type=jnp.float32
            )
            key_clip = key_clip_ref[low + j]
            for part in (slice(0, HD), slice(HD, 2 * HD)):
                masked = jnp.where(query_clip == key_clip[:, part], product[:, part], -1e30)
                peak = masked if peak is None else jnp.maximum(peak, masked)
                scores.append(masked)
        peak = jnp.broadcast_to(jnp.max(peak, axis=1, keepdims=True), (ROWS, HD))
        return low, scores, peak

    def blend(index, count, low, scores, peak):
        totals, blended = 0.0, 0.0
        for j in range(count):
            left = jnp.exp2((scores[2 * j] - peak) * SCALE)
            right = jnp.exp2((scores[2 * j + 1] - peak) * SCALE)
            totals = totals + (left + right)
            rounded = jnp.concatenate([left, right], axis=1).astype(jnp.bfloat16)
            values = rows_ref[pl.ds(2 * (low + j), 2), 2].reshape(ROWS, HD)
            blended = blended + jnp.dot(rounded, values, preferred_element_type=jnp.float32)
        result = blended / jnp.sum(totals, axis=1, keepdims=True)
        out_ref[pl.ds(2 * index, 2), 0:HD, :] = result.astype(jnp.bfloat16).reshape(2, HD, HD)

    def pair(number, carry):
        def width(count):
            def run():
                first = score(2 * number, count)
                second = score(2 * number + 1, count)
                blend(2 * number, count, *first)
                blend(2 * number + 1, count, *second)

            return run

        for choice, count in enumerate(WIDTHS):
            pl.when(pick_ref[number] == choice)(width(count))
        return carry

    lax.fori_loop(0, BLOCKS // 2, pair, 0)


def plan_kernel(edge_ref, clip_ref, low_ref, pick_ref, query_clip_ref):
    clip = clip_ref[...]

    def number(mask):
        return jnp.sum(jnp.where(mask, 1.0, 0.0)).astype(jnp.int32)

    for pair in range(BLOCKS // 2):
        lows, needs = [], []
        for index in (2 * pair, 2 * pair + 1):
            first, last = edge_ref[0, index * ROWS], edge_ref[0, (index + 1) * ROWS - 1]
            low = number(clip < first) >> 8
            lows.append(low)
            needs.append(((number(clip <= last) + ROWS - 1) >> 8) - low)
        need = jnp.maximum(needs[0], needs[1])
        pick, count = jnp.int32(0), jnp.int32(WIDTHS[0])
        for choice, width in enumerate(WIDTHS[:-1]):
            pick = jnp.where(need > width, choice + 1, pick)
            count = jnp.where(need > width, WIDTHS[choice + 1], count)
        pick_ref[pair] = pick
        for index, low in zip((2 * pair, 2 * pair + 1), lows):
            low_ref[index] = jnp.minimum(low, BLOCKS - count)
    for index in range(BLOCKS):
        row = jnp.broadcast_to(clip[index : index + 1], (HD, ROWS))
        query_clip_ref[index * ROWS : (index + 1) * ROWS, :] = jnp.transpose(row)


def stay_plan(clip):
    smem, vmem = pl.BlockSpec(memory_space=pltpu.SMEM), pl.BlockSpec(memory_space=pltpu.VMEM)
    blocks = clip.reshape(BLOCKS, ROWS)
    low, pick, query_clip = pl.pallas_call(
        plan_kernel,
        out_shape=[
            jax.ShapeDtypeStruct((BLOCKS,), jnp.int32),
            jax.ShapeDtypeStruct((BLOCKS // 2,), jnp.int32),
            jax.ShapeDtypeStruct((BLOCKS * ROWS, HD), jnp.int32),
        ],
        in_specs=[smem, vmem],
        out_specs=[smem, smem, vmem],
        compiler_params=pltpu.CompilerParams(vmem_limit_bytes=8 * 2**20),
        cost_estimate=pl.CostEstimate(flops=10**7, bytes_accessed=2**20, transcendentals=0),
        name="stay_plan",
    )(clip, blocks)
    return low, pick, blocks.reshape(BLOCKS, 1, ROWS), query_clip


def stay_attention(plan, rows):
    smem, vmem = pl.BlockSpec(memory_space=pltpu.SMEM), pl.BlockSpec(memory_space=pltpu.VMEM)
    return pl.pallas_call(
        stay_kernel,
        out_shape=jax.ShapeDtypeStruct((HEADS, HD + 8, HD), jnp.bfloat16),
        in_specs=[smem, smem, vmem, vmem, vmem],
        out_specs=vmem,
        compiler_params=pltpu.CompilerParams(vmem_limit_bytes=40 * 2**20),
        name="stay_attention",
    )(plan[0], plan[1], rows, plan[2], plan[3])


def split_kernel(length_ref, rows_ref, heads_ref, mask_ref):
    for head in range(HEADS):
        heads_ref[head, 0] = rows_ref[0, :, head * HD : (head + 1) * HD]

    @pl.when(pl.program_id(0) == 0)
    def _():
        group = lax.axis_index("x") * 8 + lax.axis_index("z")
        first, second = length_ref[2 * group], length_ref[2 * group + 1]

        def limits(axis):
            row = lax.broadcasted_iota(jnp.int32, (2 * HALF, 2 * HALF), axis)
            return row // HALF, row % HALF < jnp.where(row < HALF, first, second)

        query_half, query_usable = limits(0)
        key_half, key_usable = limits(1)
        allowed = (query_half == key_half) & query_usable & key_usable
        mask_ref[0] = jnp.where(query_usable, 1.0, 0.0)
        mask_ref[1] = jnp.where(allowed, 0.0, 1.0)


def split_heads(out_len, rows):
    return pl.pallas_call(
        split_kernel,
        grid=(3,),
        out_shape=[
            jax.ShapeDtypeStruct((HEADS, 3, HD, HD), rows.dtype),
            jax.ShapeDtypeStruct((2, 2 * HALF, 2 * HALF), jnp.float32),
        ],
        in_specs=[
            pl.BlockSpec(memory_space=pltpu.SMEM),
            pl.BlockSpec((1, HD, HEADS * HD), lambda t: (t, 0, 0)),
        ],
        out_specs=[
            pl.BlockSpec((HEADS, 1, HD, HD), lambda t: (0, t, 0, 0)),
            pl.BlockSpec((2, 2 * HALF, 2 * HALF), lambda t: (0, 0, 0)),
        ],
        compiler_params=pltpu.CompilerParams(vmem_limit_bytes=48 * 2**20),
        name="split_heads",
    )(out_len, rows)


def merge_kernel(back_ref, stay_ref, inbox_ref):
    for head in range(HEADS):
        columns = slice(head * HD, (head + 1) * HD)
        stay_ref[:, columns] = back_ref[head, 0:HD, :]
        inbox_ref[:, columns] = back_ref[head, HD : HD + 8, :]


def merge_heads(back):
    return pl.pallas_call(
        merge_kernel,
        out_shape=[
            jax.ShapeDtypeStruct((HD, HEADS * HD), back.dtype),
            jax.ShapeDtypeStruct((8, HEADS * HD), back.dtype),
        ],
        in_specs=[pl.BlockSpec(memory_space=pltpu.VMEM)],
        out_specs=[pl.BlockSpec(memory_space=pltpu.VMEM)] * 2,
        compiler_params=pltpu.CompilerParams(vmem_limit_bytes=8 * 2**20),
        name="merge_heads",
    )(back)


def box_attention(masks, rows):
    usable, blocked = masks
    queries, keys, values = (rows[:, t].reshape(2 * HALF, HD) for t in range(3))
    scores = lax.dot_general(
        queries, keys, (((1,), (1,)), ((), ())), preferred_element_type=jnp.float32
    )
    scores = jnp.where(blocked > 0.0, -1e30, scores)
    weights = jnp.exp2((scores - jnp.max(scores, axis=1, keepdims=True)) * SCALE)
    totals = jnp.sum(weights, axis=1, keepdims=True)
    blended = jnp.dot(weights.astype(jnp.bfloat16), values, preferred_element_type=jnp.float32)
    result = jnp.where(usable > 0.0, blended / totals, 0.0).astype(jnp.bfloat16)
    return with_layout_constraint(result, Layout(major_to_minor=(0, 1)))


def select_kernel(place_ref, gathered_ref, keep_ref, send_ref):
    x, z, c = lax.axis_index("x"), lax.axis_index("z"), lax.axis_index("c")
    keep_ref[...] = jnp.zeros_like(keep_ref)
    send_ref[...] = jnp.zeros_like(send_ref)
    for source in range(16):
        place = place_ref[2 * ((source // 2) * 8 + z) + source % 2]
        far = (place // 2) % 8 ^ z
        slot = (far // 2 % 2) * 4 + (far // 4) * 2 + place % 2
        mine = place // 16 == x
        for odd, slots_ref in enumerate((keep_ref, send_ref)):

            @pl.when(mine & (far % 2 == odd))
            def _(source=source, slot=slot, slots_ref=slots_ref):
                slots_ref[slot] = gathered_ref[2 * (source // 2) + c, source % 2]


def select(place, gathered):
    smem, vmem = pl.BlockSpec(memory_space=pltpu.SMEM), pl.BlockSpec(memory_space=pltpu.VMEM)
    return pl.pallas_call(
        select_kernel,
        out_shape=[jax.ShapeDtypeStruct((8, HALF, HD), jnp.bfloat16)] * 2,
        in_specs=[smem, vmem],
        out_specs=[vmem] * 2,
        compiler_params=pltpu.CompilerParams(vmem_limit_bytes=4 * 2**20),
        name="select_clips",
    )(place, gathered)


def swap(rows, bit):
    return lax.ppermute(rows, "z", [(i, i ^ bit) for i in range(8)])


def local(stay_qkv, outbox_qkv, stay_clip, out_len, out_place):
    box = jnp.transpose(outbox_qkv[0].reshape(8, 3, HEADS, HD), (2, 1, 0, 3))
    box = with_layout_constraint(box.reshape(HEADS, 24, HD), Layout(major_to_minor=(0, 1, 2)))
    box = lax.all_to_all(box, SP, split_axis=0, concat_axis=0, tiled=True)
    stay, masks = split_heads(out_len, jnp.transpose(stay_qkv[0], (1, 0, 2)))
    box, stay = lax.optimization_barrier((box, stay))
    stay = lax.all_to_all(
        stay.reshape(HEADS, 3 * HD, HD), SP, split_axis=0, concat_axis=0, tiled=True
    )

    box_out = box_attention(masks, box.reshape(HEADS, 3, 8, HD))

    gathered = lax.all_gather(box_out, ("x", "c"), axis=0, tiled=True)
    keep, send = select(out_place, gathered.reshape(16, 2, HALF, HD))
    send, clip = lax.optimization_barrier((send, stay_clip))
    came, plan = lax.optimization_barrier((swap(send, 1), stay_plan(clip)))
    slots = keep + came
    came = swap(slots[4:], 2)
    slots = slots[:4] + came
    came = swap(slots[2:], 4)

    out = stay_attention(plan, stay.reshape(HEADS, 3, HD, HD))
    out, slots = lax.optimization_barrier((out, slots))
    inbox = (slots[:2] + came).reshape(HEADS, 8, HD)
    out = lax.dynamic_update_slice(out, inbox, (0, HD, 0))
    stay_back, inbox_back = merge_heads(
        lax.all_to_all(out, SP, split_axis=0, concat_axis=0, tiled=True)
    )
    return stay_back[None], inbox_back[None]


def solution(mesh):
    lines = Mesh(mesh.devices.reshape(8, 8, 8, 2), ("x", "z", "y", "c"))
    in_specs = (P(GRP, SP, None, None), P(GRP, SP, None, None), P(GRP, None), P(), P())
    out_specs = (P(GRP, SP, None), P(GRP, SP, None))
    return jax.shard_map(local, mesh=lines, in_specs=in_specs, out_specs=out_specs, check_vma=False)
```

```python
import math

import jax
import jax.numpy as jnp
from jax import lax
from jax.experimental import pallas as pl
from jax.experimental.layout import Layout, with_layout_constraint
from jax.experimental.pallas import tpu as pltpu
from jax.sharding import Mesh
from jax.sharding import PartitionSpec as P

HEADS = 16
HD = 128
HALF = 64
ROWS = 256
BLOCKS = 8
WIDTHS = (2, 3, 4, 5, 6, 8)
SCALE = math.log2(math.e) / math.sqrt(HD)
GRP = ("x", "z")
SP = ("y", "c")


def stay_kernel(low_ref, pick_ref, rows_ref, key_clip_ref, query_clip_ref, out_ref):
    def score(index, count):
        queries = rows_ref[pl.ds(2 * index, 2), 0].reshape(ROWS, HD)
        query_clip = query_clip_ref[pl.ds(pl.multiple_of(index * ROWS, ROWS), ROWS), :]
        low = low_ref[index]
        scores, peak = [], None
        for j in range(count):
            keys = rows_ref[pl.ds(2 * (low + j), 2), 1].reshape(ROWS, HD)
            product = lax.dot_general(
                queries, keys, (((1,), (1,)), ((), ())), preferred_element_type=jnp.float32
            )
            key_clip = key_clip_ref[:, pl.ds(pl.multiple_of((low + j) * ROWS, ROWS), ROWS)]
            for part in (slice(0, HD), slice(HD, 2 * HD)):
                masked = jnp.where(query_clip == key_clip[:, part], product[:, part], -1e30)
                peak = masked if peak is None else jnp.maximum(peak, masked)
                scores.append(masked)
        peak = jnp.broadcast_to(jnp.max(peak, axis=1, keepdims=True), (ROWS, HD))
        return low, scores, peak

    def blend(index, count, low, scores, peak):
        totals, blended = 0.0, 0.0
        for j in range(count):
            left = jnp.exp2((scores[2 * j] - peak) * SCALE)
            right = jnp.exp2((scores[2 * j + 1] - peak) * SCALE)
            totals = totals + (left + right)
            rounded = jnp.concatenate([left, right], axis=1).astype(jnp.bfloat16)
            values = rows_ref[pl.ds(2 * (low + j), 2), 2].reshape(ROWS, HD)
            blended = blended + jnp.dot(rounded, values, preferred_element_type=jnp.float32)
        result = blended / jnp.sum(totals, axis=1, keepdims=True)
        out_ref[pl.ds(2 * index, 2), 0:HD, :] = result.astype(jnp.bfloat16).reshape(2, HD, HD)

    def pair(number, carry):
        def width(count):
            def run():
                first = score(2 * number, count)
                second = score(2 * number + 1, count)
                blend(2 * number, count, *first)
                blend(2 * number + 1, count, *second)

            return run

        for choice, count in enumerate(WIDTHS):
            pl.when(pick_ref[number] == choice)(width(count))
        return carry

    lax.fori_loop(0, BLOCKS // 2, pair, 0)


def plan_kernel(edge_ref, clip_ref, low_ref, pick_ref, query_clip_ref):
    clip = clip_ref[...]

    def number(mask):
        return jnp.sum(jnp.where(mask, 1.0, 0.0)).astype(jnp.int32)

    for pair in range(BLOCKS // 2):
        lows, needs = [], []
        for index in (2 * pair, 2 * pair + 1):
            first, last = edge_ref[0, index * ROWS], edge_ref[0, (index + 1) * ROWS - 1]
            low = number(clip < first) >> 8
            lows.append(low)
            needs.append(((number(clip <= last) + ROWS - 1) >> 8) - low)
        need = jnp.maximum(needs[0], needs[1])
        pick, count = jnp.int32(0), jnp.int32(WIDTHS[0])
        for choice, width in enumerate(WIDTHS[:-1]):
            pick = jnp.where(need > width, choice + 1, pick)
            count = jnp.where(need > width, WIDTHS[choice + 1], count)
        pick_ref[pair] = pick
        for index, low in zip((2 * pair, 2 * pair + 1), lows):
            low_ref[index] = jnp.minimum(low, BLOCKS - count)
    for index in range(BLOCKS):
        row = jnp.broadcast_to(clip[:, index * ROWS : (index + 1) * ROWS], (HD, ROWS))
        query_clip_ref[index * ROWS : (index + 1) * ROWS, :] = jnp.transpose(row)


def stay_plan(clip):
    smem, vmem = pl.BlockSpec(memory_space=pltpu.SMEM), pl.BlockSpec(memory_space=pltpu.VMEM)
    low, pick, query_clip = pl.pallas_call(
        plan_kernel,
        out_shape=[
            jax.ShapeDtypeStruct((BLOCKS,), jnp.int32),
            jax.ShapeDtypeStruct((BLOCKS // 2,), jnp.int32),
            jax.ShapeDtypeStruct((BLOCKS * ROWS, HD), jnp.int32),
        ],
        in_specs=[smem, vmem],
        out_specs=[smem, smem, vmem],
        compiler_params=pltpu.CompilerParams(vmem_limit_bytes=8 * 2**20),
        cost_estimate=pl.CostEstimate(flops=10**7, bytes_accessed=2**20, transcendentals=0),
        name="stay_plan",
    )(clip, clip)
    return low, pick, clip, query_clip


def stay_attention(plan, rows):
    smem, vmem = pl.BlockSpec(memory_space=pltpu.SMEM), pl.BlockSpec(memory_space=pltpu.VMEM)
    return pl.pallas_call(
        stay_kernel,
        out_shape=jax.ShapeDtypeStruct((HEADS, HD + 8, HD), jnp.bfloat16),
        in_specs=[smem, smem, vmem, vmem, vmem],
        out_specs=vmem,
        compiler_params=pltpu.CompilerParams(vmem_limit_bytes=40 * 2**20),
        name="stay_attention",
    )(plan[0], plan[1], rows, plan[2], plan[3])


def split_kernel(length_ref, rows_ref, heads_ref, mask_ref):
    for head in range(HEADS):
        heads_ref[head, 0] = rows_ref[0, :, head * HD : (head + 1) * HD]

    @pl.when(pl.program_id(0) == 0)
    def _():
        group = lax.axis_index("x") * 8 + lax.axis_index("z")
        first, second = length_ref[2 * group], length_ref[2 * group + 1]

        def limits(axis):
            row = lax.broadcasted_iota(jnp.int32, (2 * HALF, 2 * HALF), axis)
            return row // HALF, row % HALF < jnp.where(row < HALF, first, second)

        query_half, query_usable = limits(0)
        key_half, key_usable = limits(1)
        allowed = (query_half == key_half) & query_usable & key_usable
        mask_ref[0] = jnp.where(query_usable, 1.0, 0.0)
        mask_ref[1] = jnp.where(allowed, 0.0, 1.0)


def split_heads(out_len, rows):
    return pl.pallas_call(
        split_kernel,
        grid=(3,),
        out_shape=[
            jax.ShapeDtypeStruct((HEADS, 3, HD, HD), rows.dtype),
            jax.ShapeDtypeStruct((2, 2 * HALF, 2 * HALF), jnp.float32),
        ],
        in_specs=[
            pl.BlockSpec(memory_space=pltpu.SMEM),
            pl.BlockSpec((1, HD, HEADS * HD), lambda t: (t, 0, 0)),
        ],
        out_specs=[
            pl.BlockSpec((HEADS, 1, HD, HD), lambda t: (0, t, 0, 0)),
            pl.BlockSpec((2, 2 * HALF, 2 * HALF), lambda t: (0, 0, 0)),
        ],
        name="split_heads",
    )(out_len, rows)


def merge_kernel(back_ref, stay_ref, inbox_ref):
    for head in range(HEADS):
        columns = slice(head * HD, (head + 1) * HD)
        stay_ref[:, columns] = back_ref[head, 0:HD, :]
        inbox_ref[:, columns] = back_ref[head, HD : HD + 8, :]


def merge_heads(back):
    return pl.pallas_call(
        merge_kernel,
        out_shape=[
            jax.ShapeDtypeStruct((HD, HEADS * HD), back.dtype),
            jax.ShapeDtypeStruct((8, HEADS * HD), back.dtype),
        ],
        in_specs=[pl.BlockSpec(memory_space=pltpu.VMEM)],
        out_specs=[pl.BlockSpec(memory_space=pltpu.VMEM)] * 2,
        compiler_params=pltpu.CompilerParams(vmem_limit_bytes=8 * 2**20),
        name="merge_heads",
    )(back)


def box_attention(masks, rows):
    usable, blocked = masks
    queries, keys, values = (rows[:, t].reshape(2 * HALF, HD) for t in range(3))
    scores = lax.dot_general(
        queries, keys, (((1,), (1,)), ((), ())), preferred_element_type=jnp.float32
    )
    scores = jnp.where(blocked > 0.0, -1e30, scores)
    weights = jnp.exp2((scores - jnp.max(scores, axis=1, keepdims=True)) * SCALE)
    totals = jnp.sum(weights, axis=1, keepdims=True)
    blended = jnp.dot(weights.astype(jnp.bfloat16), values, preferred_element_type=jnp.float32)
    result = jnp.where(usable > 0.0, blended / totals, 0.0).astype(jnp.bfloat16)
    return with_layout_constraint(result, Layout(major_to_minor=(0, 1)))


def select_kernel(place_ref, gathered_ref, *slot_refs):
    x, z, c = lax.axis_index("x"), lax.axis_index("z"), lax.axis_index("c")
    for slot_ref in slot_refs:
        slot_ref[...] = jnp.zeros_like(slot_ref)
    for source in range(16):
        place = place_ref[2 * ((source // 2) * 8 + z) + source % 2]
        far = (place // 2) % 8 ^ z
        slot = (far // 4) * 2 + place % 2
        near = jnp.where(place // 16 == x, far % 4, -1)
        for u, slot_ref in enumerate(slot_refs):

            @pl.when(near == u)
            def _(source=source, slot=slot, slot_ref=slot_ref):
                slot_ref[slot] = gathered_ref[2 * (source // 2) + c, source % 2]


def select(place, gathered):
    smem, vmem = pl.BlockSpec(memory_space=pltpu.SMEM), pl.BlockSpec(memory_space=pltpu.VMEM)
    return pl.pallas_call(
        select_kernel,
        out_shape=[jax.ShapeDtypeStruct((4, HALF, HD), jnp.bfloat16)] * 4,
        in_specs=[smem, vmem],
        out_specs=[vmem] * 4,
        compiler_params=pltpu.CompilerParams(vmem_limit_bytes=4 * 2**20),
        name="select_clips",
    )(place, gathered)


def swap(rows, bit):
    return lax.ppermute(rows, "z", [(i, i ^ bit) for i in range(8)])


def local(stay_qkv, outbox_qkv, stay_clip, out_len, out_place):
    box = jnp.transpose(outbox_qkv[0].reshape(8, 3, HEADS, HD), (2, 1, 0, 3))
    box = with_layout_constraint(box.reshape(HEADS, 24, HD), Layout(major_to_minor=(0, 1, 2)))
    box = lax.all_to_all(box, SP, split_axis=0, concat_axis=0, tiled=True)
    stay, masks = split_heads(out_len, jnp.transpose(stay_qkv[0], (1, 0, 2)))
    box, stay = lax.optimization_barrier((box, stay))
    stay = lax.all_to_all(
        stay.reshape(HEADS, 3 * HD, HD), SP, split_axis=0, concat_axis=0, tiled=True
    )

    box_out = box_attention(masks, box.reshape(HEADS, 3, 8, HD))

    gathered = lax.all_gather(box_out, ("x", "c"), axis=0, tiled=True)
    slots = select(out_place, gathered.reshape(16, 2, HALF, HD))
    slots, clip = lax.optimization_barrier((slots, stay_clip))
    came = swap(slots[3], 3), swap(slots[2], 2), swap(slots[1], 1)
    came, plan = lax.optimization_barrier((came, stay_plan(clip)))
    slots = slots[0] + came[0] + came[1] + came[2]
    came = swap(slots[2:], 4)

    out = stay_attention(plan, stay.reshape(HEADS, 3, HD, HD))
    out, slots = lax.optimization_barrier((out, slots))
    inbox = (slots[:2] + came).reshape(HEADS, 8, HD)
    out = lax.dynamic_update_slice(out, inbox, (0, HD, 0))
    stay_back, inbox_back = merge_heads(
        lax.all_to_all(out, SP, split_axis=0, concat_axis=0, tiled=True)
    )
    return stay_back[None], inbox_back[None]


def solution(mesh):
    lines = Mesh(mesh.devices.reshape(8, 8, 8, 2), ("x", "z", "y", "c"))
    in_specs = (P(GRP, SP, None, None), P(GRP, SP, None, None), P(GRP, None), P(), P())
    out_specs = (P(GRP, SP, None), P(GRP, SP, None))
    return jax.shard_map(local, mesh=lines, in_specs=in_specs, out_specs=out_specs, check_vma=False)
```

```python
import math

import jax
import jax.numpy as jnp
from jax import lax
from jax.experimental import pallas as pl
from jax.experimental.layout import Layout, with_layout_constraint
from jax.experimental.pallas import tpu as pltpu
from jax.sharding import Mesh
from jax.sharding import PartitionSpec as P

HEADS = 16
HD = 128
HALF = 64
ROWS = 256
BLOCKS = 8
WIDTHS = (2, 3, 4, 5, 6, 8)
SCALE = math.log2(math.e) / math.sqrt(HD)
GRP = ("x", "z")
SP = ("y", "c")


def stay_kernel(low_ref, pick_ref, rows_ref, key_clip_ref, query_clip_ref, out_ref):
    def score(index, count):
        queries = rows_ref[pl.ds(2 * index, 2), 0].reshape(ROWS, HD)
        query_clip = query_clip_ref[pl.ds(pl.multiple_of(index * ROWS, ROWS), ROWS), :]
        low = low_ref[index]
        scores, peak = [], None
        for j in range(count):
            keys = rows_ref[pl.ds(2 * (low + j), 2), 1].reshape(ROWS, HD)
            product = lax.dot_general(
                queries, keys, (((1,), (1,)), ((), ())), preferred_element_type=jnp.float32
            )
            key_clip = key_clip_ref[:, pl.ds(pl.multiple_of((low + j) * ROWS, ROWS), ROWS)]
            for part in (slice(0, HD), slice(HD, 2 * HD)):
                masked = jnp.where(query_clip == key_clip[:, part], product[:, part], -1e30)
                peak = masked if peak is None else jnp.maximum(peak, masked)
                scores.append(masked)
        peak = jnp.broadcast_to(jnp.max(peak, axis=1, keepdims=True), (ROWS, HD))
        return low, scores, peak

    def blend(index, count, low, scores, peak):
        totals, blended = 0.0, 0.0
        for j in range(count):
            left = jnp.exp2((scores[2 * j] - peak) * SCALE)
            right = jnp.exp2((scores[2 * j + 1] - peak) * SCALE)
            totals = totals + (left + right)
            rounded = jnp.concatenate([left, right], axis=1).astype(jnp.bfloat16)
            values = rows_ref[pl.ds(2 * (low + j), 2), 2].reshape(ROWS, HD)
            blended = blended + jnp.dot(rounded, values, preferred_element_type=jnp.float32)
        result = blended / jnp.sum(totals, axis=1, keepdims=True)
        out_ref[pl.ds(2 * index, 2), 0:HD, :] = result.astype(jnp.bfloat16).reshape(2, HD, HD)

    def pair(number, carry):
        def width(count):
            def run():
                first = score(2 * number, count)
                second = score(2 * number + 1, count)
                blend(2 * number, count, *first)
                blend(2 * number + 1, count, *second)

            return run

        for choice, count in enumerate(WIDTHS):
            pl.when(pick_ref[number] == choice)(width(count))
        return carry

    lax.fori_loop(0, BLOCKS // 2, pair, 0)


def plan_kernel(edge_ref, clip_ref, low_ref, pick_ref, query_clip_ref):
    clip = clip_ref[...]

    def number(mask):
        return jnp.sum(jnp.where(mask, 1.0, 0.0)).astype(jnp.int32)

    for pair in range(BLOCKS // 2):
        lows, needs = [], []
        for index in (2 * pair, 2 * pair + 1):
            first, last = edge_ref[0, index * ROWS], edge_ref[0, (index + 1) * ROWS - 1]
            low = number(clip < first) >> 8
            lows.append(low)
            needs.append(((number(clip <= last) + ROWS - 1) >> 8) - low)
        need = jnp.maximum(needs[0], needs[1])
        pick, count = jnp.int32(0), jnp.int32(WIDTHS[0])
        for choice, width in enumerate(WIDTHS[:-1]):
            pick = jnp.where(need > width, choice + 1, pick)
            count = jnp.where(need > width, WIDTHS[choice + 1], count)
        pick_ref[pair] = pick
        for index, low in zip((2 * pair, 2 * pair + 1), lows):
            low_ref[index] = jnp.minimum(low, BLOCKS - count)
    for index in range(BLOCKS):
        row = jnp.broadcast_to(clip[:, index * ROWS : (index + 1) * ROWS], (HD, ROWS))
        query_clip_ref[index * ROWS : (index + 1) * ROWS, :] = jnp.transpose(row)


def stay_plan(clip):
    smem, vmem = pl.BlockSpec(memory_space=pltpu.SMEM), pl.BlockSpec(memory_space=pltpu.VMEM)
    low, pick, query_clip = pl.pallas_call(
        plan_kernel,
        out_shape=[
            jax.ShapeDtypeStruct((BLOCKS,), jnp.int32),
            jax.ShapeDtypeStruct((BLOCKS // 2,), jnp.int32),
            jax.ShapeDtypeStruct((BLOCKS * ROWS, HD), jnp.int32),
        ],
        in_specs=[smem, vmem],
        out_specs=[smem, smem, vmem],
        compiler_params=pltpu.CompilerParams(vmem_limit_bytes=8 * 2**20),
        cost_estimate=pl.CostEstimate(flops=10**7, bytes_accessed=2**20, transcendentals=0),
        name="stay_plan",
    )(clip, clip)
    return low, pick, clip, query_clip


def stay_attention(plan, rows):
    smem, vmem = pl.BlockSpec(memory_space=pltpu.SMEM), pl.BlockSpec(memory_space=pltpu.VMEM)
    return pl.pallas_call(
        stay_kernel,
        out_shape=jax.ShapeDtypeStruct((HEADS, HD + 8, HD), jnp.bfloat16),
        in_specs=[smem, smem, vmem, vmem, vmem],
        out_specs=vmem,
        compiler_params=pltpu.CompilerParams(vmem_limit_bytes=40 * 2**20),
        name="stay_attention",
    )(plan[0], plan[1], rows, plan[2], plan[3])


def split_kernel(length_ref, rows_ref, heads_ref, mask_ref):
    for head in range(HEADS):
        heads_ref[head, 0] = rows_ref[0, :, head * HD : (head + 1) * HD]

    @pl.when(pl.program_id(0) == 0)
    def _():
        group = lax.axis_index("x") * 8 + lax.axis_index("z")
        first, second = length_ref[2 * group], length_ref[2 * group + 1]

        def limits(axis):
            row = lax.broadcasted_iota(jnp.int32, (2 * HALF, 2 * HALF), axis)
            return row // HALF, row % HALF < jnp.where(row < HALF, first, second)

        query_half, query_usable = limits(0)
        key_half, key_usable = limits(1)
        allowed = (query_half == key_half) & query_usable & key_usable
        mask_ref[0] = jnp.where(query_usable, 1.0, 0.0)
        mask_ref[1] = jnp.where(allowed, 0.0, 1.0)


def split_heads(out_len, rows):
    return pl.pallas_call(
        split_kernel,
        grid=(3,),
        out_shape=[
            jax.ShapeDtypeStruct((HEADS, 3, HD, HD), rows.dtype),
            jax.ShapeDtypeStruct((2, 2 * HALF, 2 * HALF), jnp.float32),
        ],
        in_specs=[
            pl.BlockSpec(memory_space=pltpu.SMEM),
            pl.BlockSpec((1, HD, HEADS * HD), lambda t: (t, 0, 0)),
        ],
        out_specs=[
            pl.BlockSpec((HEADS, 1, HD, HD), lambda t: (0, t, 0, 0)),
            pl.BlockSpec((2, 2 * HALF, 2 * HALF), lambda t: (0, 0, 0)),
        ],
        name="split_heads",
    )(out_len, rows)


def merge_kernel(back_ref, stay_ref, inbox_ref):
    for head in range(HEADS):
        columns = slice(head * HD, (head + 1) * HD)
        stay_ref[:, columns] = back_ref[head, 0:HD, :]
        inbox_ref[:, columns] = back_ref[head, HD : HD + 8, :]


def merge_heads(back):
    return pl.pallas_call(
        merge_kernel,
        out_shape=[
            jax.ShapeDtypeStruct((HD, HEADS * HD), back.dtype),
            jax.ShapeDtypeStruct((8, HEADS * HD), back.dtype),
        ],
        in_specs=[pl.BlockSpec(memory_space=pltpu.VMEM)],
        out_specs=[pl.BlockSpec(memory_space=pltpu.VMEM)] * 2,
        compiler_params=pltpu.CompilerParams(vmem_limit_bytes=8 * 2**20),
        name="merge_heads",
    )(back)


def box_attention(masks, rows):
    usable, blocked = masks
    queries, keys, values = (rows[:, t].reshape(2 * HALF, HD) for t in range(3))
    scores = lax.dot_general(
        queries, keys, (((1,), (1,)), ((), ())), preferred_element_type=jnp.float32
    )
    scores = jnp.where(blocked > 0.0, -1e30, scores)
    weights = jnp.exp2((scores - jnp.max(scores, axis=1, keepdims=True)) * SCALE)
    totals = jnp.sum(weights, axis=1, keepdims=True)
    blended = jnp.dot(weights.astype(jnp.bfloat16), values, preferred_element_type=jnp.float32)
    result = jnp.where(usable > 0.0, blended / totals, 0.0).astype(jnp.bfloat16)
    return with_layout_constraint(result, Layout(major_to_minor=(0, 1)))


def select_kernel(place_ref, gathered_ref, *slot_refs):
    x, z, c = lax.axis_index("x"), lax.axis_index("z"), lax.axis_index("c")
    for slot_ref in slot_refs:
        slot_ref[...] = jnp.zeros_like(slot_ref)
    for source in range(16):
        place = place_ref[2 * ((source // 2) * 8 + z) + source % 2]
        far = (place // 2) % 8 ^ z
        slot = (far // 2 % 2) * 2 + place % 2
        near = jnp.where(place // 16 == x, (far // 4) * 2 + far % 2, -1)
        for u, slot_ref in enumerate(slot_refs):

            @pl.when(near == u)
            def _(source=source, slot=slot, slot_ref=slot_ref):
                slot_ref[slot] = gathered_ref[2 * (source // 2) + c, source % 2]


def select(place, gathered):
    smem, vmem = pl.BlockSpec(memory_space=pltpu.SMEM), pl.BlockSpec(memory_space=pltpu.VMEM)
    return pl.pallas_call(
        select_kernel,
        out_shape=[jax.ShapeDtypeStruct((4, HALF, HD), jnp.bfloat16)] * 4,
        in_specs=[smem, vmem],
        out_specs=[vmem] * 4,
        compiler_params=pltpu.CompilerParams(vmem_limit_bytes=4 * 2**20),
        name="select_clips",
    )(place, gathered)


def swap(rows, bit):
    return lax.ppermute(rows, "z", [(i, i ^ bit) for i in range(8)])


def local(stay_qkv, outbox_qkv, stay_clip, out_len, out_place):
    box = jnp.transpose(outbox_qkv[0].reshape(8, 3, HEADS, HD), (2, 1, 0, 3))
    box = with_layout_constraint(box.reshape(HEADS, 24, HD), Layout(major_to_minor=(0, 1, 2)))
    box = lax.all_to_all(box, SP, split_axis=0, concat_axis=0, tiled=True)
    stay, masks = split_heads(out_len, jnp.transpose(stay_qkv[0], (1, 0, 2)))
    box, stay = lax.optimization_barrier((box, stay))
    stay = lax.all_to_all(
        stay.reshape(HEADS, 3 * HD, HD), SP, split_axis=0, concat_axis=0, tiled=True
    )

    box_out = box_attention(masks, box.reshape(HEADS, 3, 8, HD))

    gathered = lax.all_gather(box_out, ("x", "c"), axis=0, tiled=True)
    slots = select(out_place, gathered.reshape(16, 2, HALF, HD))
    slots, clip = lax.optimization_barrier((slots, stay_clip))
    came = swap(slots[2], 4), swap(slots[3], 5), swap(slots[1], 1)
    came, plan = lax.optimization_barrier((came, stay_plan(clip)))
    slots = slots[0] + came[0] + came[1] + came[2]
    came = swap(slots[2:], 2)

    out = stay_attention(plan, stay.reshape(HEADS, 3, HD, HD))
    out, slots = lax.optimization_barrier((out, slots))
    inbox = (slots[:2] + came).reshape(HEADS, 8, HD)
    out = lax.dynamic_update_slice(out, inbox, (0, HD, 0))
    stay_back, inbox_back = merge_heads(
        lax.all_to_all(out, SP, split_axis=0, concat_axis=0, tiled=True)
    )
    return stay_back[None], inbox_back[None]


def solution(mesh):
    lines = Mesh(mesh.devices.reshape(8, 8, 8, 2), ("x", "z", "y", "c"))
    in_specs = (P(GRP, SP, None, None), P(GRP, SP, None, None), P(GRP, None), P(), P())
    out_specs = (P(GRP, SP, None), P(GRP, SP, None))
    return jax.shard_map(local, mesh=lines, in_specs=in_specs, out_specs=out_specs, check_vma=False)
```
